512 devices in a mesh: row: 16 (over y_hi, x, core), col: 32 (over z, y_lo).
Axes of the slice: x: 4, y: 4 (y_hi: 2, y_lo: 2; y = y_hi * 2 + y_lo), z: 16, core: 2. Of those that a mesh axis runs over, the one named last changes fastest.
Arguments:
- object_field: float32 [2, 4096, 8192], P(None, 'row', 'col'), may hold values from -6 to 6
- probe_field: float32 [2, 256, 256], replicated, may hold values from -4 to 4
- intensity: float32 [16, 32, 6, 256, 256], P('row', 'col'), may hold values from 0.05 to 2
- positions: int32 [16, 32, 6, 2], P('row', 'col'), may hold values from -128 to 127
- counts: int32 [16, 32], P('row', 'col'), may hold values from 1 to 6, as said below
Outputs:
- object_new: float32 [2, 4096, 8192], P(None, 'row', 'col')
- probe_update: float32 [2, 256, 256], replicated
The draws below stay inside these ranges and needn't reach their ends.
Inputs may be any that keep to these rules, and one draw needn't show every extreme that they name: Slots at or after counts of a tile are padding and are ignored; some tile has exactly 6 live slots. `positions`: each window's first pixel lies within 128 pixels before or inside its tile, so windows reach only the eight neighbouring tiles.
All inputs are finite; a program needn't handle non-finite values.
Results may differ from the reference program's by a relative error of at most 0.0003.
Values sent between devices are 32-bit elements; how exact they have to be, the bound alone decides.
No kernel may reach another device: no remote copies, remote signals or barrier semaphores. Data moves between devices by JAX's collectives and lax.ppermute only.
A program may use at most 64 MiB of HBM per device.

```python
import math
import jax
import jax.numpy as jnp
from jax import lax

PROBE_SIDE = 256
TILE_SIDE = 256
SLOT_COUNT = 6
RIM_WIDTH = 128
GRID_ROWS = 16
GRID_COLS = 32
OBJECT_ROWS = 4096
OBJECT_COLS = 8192


def draw_counts(key, part):
    key_lower, key_other, key_row, key_col = jax.random.split(key, 4)
    lower = jax.random.randint(key_lower, (GRID_ROWS, GRID_COLS), 1, SLOT_COUNT + 1)
    other = jax.random.randint(key_other, (GRID_ROWS, GRID_COLS), 1, SLOT_COUNT + 1)
    drawn = jnp.minimum(lower, other)
    pick_row = jax.random.randint(key_row, (), 0, GRID_ROWS)
    pick_col = jax.random.randint(key_col, (), 0, GRID_COLS)
    return drawn.at[pick_row, pick_col].set(SLOT_COUNT).astype(jnp.int32)


def with_ends(values, key, low, top_value):
    shape = values.shape
    index_at = [jax.random.randint(jax.random.fold_in(key, axis), (), 0, shape[axis]) for axis in range(len(shape))]
    values = values.at[tuple(index_at)].set(low)
    longest = shape.index(max(shape))
    index_at[longest] = (index_at[longest] + 1) % shape[longest]
    return values.at[tuple(index_at)].set(top_value)


def block_scale(own_key, dims, pieces, smallest, largest):
    level = 1.0
    for axis_at, parts in pieces:
        heights = jax.random.uniform(jax.random.fold_in(jax.random.fold_in(own_key, 6), axis_at), (parts,), jnp.float32, smallest / len(pieces), largest / len(pieces))
        level = level * jnp.repeat(jnp.exp(heights), dims[axis_at] // parts).reshape((-1,) + (1,) * (len(dims) - 1 - axis_at))
    return level


def noise(rng, extent, width, most, cuts=(), held_as=jnp.bfloat16):
    level = block_scale(rng, extent, cuts, -0.22, 0.18) if cuts else 1.0
    entries = jax.random.normal(rng, extent, jnp.float32) * width * level
    return jnp.minimum(jnp.maximum(entries, -most), most).astype(held_as)


def setup_inputs(seed: int = 0) -> dict:
    splits = jax.random.split(jax.random.key(seed), 6)
    return {
        "object_field": noise(splits[0], (2, OBJECT_ROWS, OBJECT_COLS), 0.7, 6.0, ((1, 16), (2, 32)), jnp.float32),
        "probe_field": noise(splits[1], (2, PROBE_SIDE, PROBE_SIDE), 0.5, 4.0, (), jnp.float32),
        "intensity": jnp.clip(jnp.exp(math.log(2.0) - 3.6888794 * jax.random.uniform(splits[2], (GRID_ROWS, GRID_COLS, SLOT_COUNT, PROBE_SIDE, PROBE_SIDE), jnp.float32) ** block_scale(splits[2], (GRID_ROWS, GRID_COLS, SLOT_COUNT, PROBE_SIDE, PROBE_SIDE), ((0, 16), (1, 32)), -0.2, 0.2)), 0.05, 2.0),
        "positions": with_ends(jax.random.randint(splits[3], (GRID_ROWS, GRID_COLS, SLOT_COUNT, 2), 0 - RIM_WIDTH, TILE_SIDE - RIM_WIDTH), jax.random.fold_in(splits[3], 1), 0 - RIM_WIDTH, (TILE_SIDE - RIM_WIDTH) - 1).astype(jnp.int32),
        "counts": draw_counts(jax.random.fold_in(splits[5], 71), 0),
    }


OBJECT_RATE = 0.5

def reference(object_field, probe_field, intensity, positions, counts):
    rim = PROBE_SIDE // 2
    padded = jnp.pad(object_field, ((0, 0), (rim, rim), (rim, rim)))
    probe_real = probe_field[0]
    probe_imag = probe_field[1]
    total_items = GRID_ROWS * GRID_COLS * SLOT_COUNT
    offsets = positions.reshape(total_items, 2).astype(jnp.int32)
    tile_rows = jnp.repeat(jnp.arange(GRID_ROWS, dtype=jnp.int32), GRID_COLS * SLOT_COUNT)
    tile_cols = jnp.tile(jnp.repeat(jnp.arange(GRID_COLS, dtype=jnp.int32), SLOT_COUNT), GRID_ROWS)
    slot_ids = jnp.tile(jnp.arange(SLOT_COUNT, dtype=jnp.int32), GRID_ROWS * GRID_COLS)
    patterns = intensity.reshape(total_items, PROBE_SIDE, PROBE_SIDE)

    def advance(totals, record):
        grad_padded, grad_probe = totals
        offset, tile_row, tile_col, slot_id, pattern = record
        active = (slot_id < counts[tile_row, tile_col]).astype(object_field.dtype)
        row_start = (tile_row * TILE_SIDE + rim + offset[0]).astype(jnp.int32)
        col_start = (tile_col * TILE_SIDE + rim + offset[1]).astype(jnp.int32)
        anchor = jnp.zeros((), jnp.int32)
        window = lax.dynamic_slice(padded, (anchor, row_start, col_start), (2, PROBE_SIDE, PROBE_SIDE))
        object_real = window[0]
        object_imag = window[1]
        exit_real = probe_real * object_real - probe_imag * object_imag
        exit_imag = probe_real * object_imag + probe_imag * object_real
        far_field = jnp.fft.fft2(exit_real + 1j * exit_imag, norm='ortho')
        far_power = far_field.real * far_field.real + far_field.imag * far_field.imag
        misfit = (far_power - pattern) * active
        back_field = jnp.fft.ifft2(far_field * misfit, norm='ortho')
        back_real = back_field.real.astype(object_field.dtype)
        back_imag = back_field.imag.astype(object_field.dtype)
        object_grad = jnp.stack([probe_real * back_real + probe_imag * back_imag, probe_real * back_imag - probe_imag * back_real])
        probe_grad = jnp.stack([object_real * back_real + object_imag * back_imag, object_real * back_imag - object_imag * back_real])
        current = lax.dynamic_slice(grad_padded, (anchor, row_start, col_start), (2, PROBE_SIDE, PROBE_SIDE))
        grad_padded = lax.dynamic_update_slice(grad_padded, current + object_grad, (anchor, row_start, col_start))
        return ((grad_padded, grad_probe + probe_grad), None)
    start_totals = (jnp.zeros_like(padded), jnp.zeros_like(probe_field))
    (grad_padded, grad_probe), _ = lax.scan(advance, start_totals, (offsets, tile_rows, tile_cols, slot_ids, patterns))
    object_gradient = grad_padded[:, rim:rim + OBJECT_ROWS, rim:rim + OBJECT_COLS]
    object_new = object_field - OBJECT_RATE * object_gradient
    probe_update = grad_probe * (1.0 / jnp.sqrt(jnp.float32(total_items)))
    return (object_new, probe_update)
```

```python
import math

import jax
import jax.numpy as jnp
import ml_dtypes
import numpy as np
from jax import lax
from jax.experimental import pallas as pl
from jax.experimental.pallas import tpu as pltpu
from jax.sharding import Mesh, PartitionSpec as P

OBJECT_RATE = 0.5
ROW = ("yh", "x", "core")
COL = ("z", "yl")
PLANE = ("yh", "x", "core", "yl")
DEEP = "z"
SIDE = 256
RIM = 128
WIDE = 2 * SIDE
F32 = jnp.float32
BF16 = jnp.bfloat16


def two_terms(table):
    high = table.astype(np.float32).astype(ml_dtypes.bfloat16)
    low = (table - high.astype(np.float64)).astype(np.float32).astype(ml_dtypes.bfloat16)
    return high, low


def spectral_tables():
    index = np.arange(SIDE)
    angles = (index[:, None] * index[None, :] % SIDE) * (2.0 * math.pi / SIDE)
    cos, sin = np.cos(angles) / 16.0, np.sin(angles) / 16.0
    out = []
    for sign in (1.0, -1.0):
        left = np.concatenate([cos, sign * sin], 1)
        right = np.block([[cos, -sign * sin], [sign * sin, cos]])
        high, low = two_terms(left)
        out.append(np.concatenate([high, high, low], 1))
        high, low = two_terms(right)
        out.append(np.concatenate([high, high, low], 0))
    return out


def split(value):
    high = value.astype(BF16)
    low = (value - high.astype(F32)).astype(BF16)
    return high, low


def slots_kernel(
    counts_ref, pos_ref, tile_ref, side_l_ref, side_r_ref, top_ref, bot_ref, ctop_ref, cbot_ref,
    probe_ref, intensity_ref, left_fwd_ref, right_fwd_ref, left_inv_ref, right_inv_ref,
    gprobe_ref, gtop_ref, gbot_ref, gmid_ref,
    ext_ref, twice_ref, shifted_ref, window_ref, stack_ref, mid_ref, back_ref,
):
    dot = lambda a, b: jnp.dot(a, b, preferred_element_type=F32)
    for c in range(2):
        ext_ref[c, RIM : RIM + SIDE, RIM : RIM + SIDE] = tile_ref[c]
        ext_ref[c, RIM : RIM + SIDE, 0:RIM] = side_l_ref[c]
        ext_ref[c, RIM : RIM + SIDE, RIM + SIDE :] = side_r_ref[c]
        ext_ref[c, 0:RIM, RIM : RIM + SIDE] = top_ref[c]
        ext_ref[c, RIM + SIDE :, RIM : RIM + SIDE] = bot_ref[c]
        ext_ref[c, 0:RIM, 0:RIM] = ctop_ref[c, :, 0:RIM]
        ext_ref[c, 0:RIM, RIM + SIDE :] = ctop_ref[c, :, RIM:]
        ext_ref[c, RIM + SIDE :, 0:RIM] = cbot_ref[c, :, 0:RIM]
        ext_ref[c, RIM + SIDE :, RIM + SIDE :] = cbot_ref[c, :, RIM:]
        twice_ref[c, 0:SIDE] = probe_ref[c]
        twice_ref[c, SIDE:WIDE] = probe_ref[c]
        gprobe_ref[c] = jnp.zeros((SIDE, SIDE), F32)
        gtop_ref[c] = jnp.zeros((RIM, WIDE), F32)
        gbot_ref[c] = jnp.zeros((RIM, WIDE), F32)
        gmid_ref[c] = jnp.zeros((SIDE, WIDE), F32)

    step = 64
    blocks = [slice(k, k + step) for k in range(0, SIDE, step)]

    def rows_from(ref, c, offset, start):
        over = offset & 7
        base = pl.multiple_of(offset - over + start, 8)
        return pltpu.roll(ref[c, pl.ds(base, step + 8), :], jnp.where(over == 0, 0, step + 8 - over), 0)[0:step]

    def put(rows, real, imag):
        real_high, real_low = split(real)
        imag_high, imag_low = split(imag)
        for base, re, im in ((0, real_high, imag_high), (WIDE, real_low, imag_low), (2 * WIDE, real_high, imag_high)):
            upper = slice(base + rows.start, base + rows.stop)
            lower = slice(base + SIDE + rows.start, base + SIDE + rows.stop)
            stack_ref[upper, 0:SIDE] = re
            stack_ref[upper, SIDE:] = im
            stack_ref[lower, 0:SIDE] = im
            stack_ref[lower, SIDE:] = -re

    def wide(value):
        high, low = split(value)
        return jnp.concatenate([high, low, high], axis=1)

    def one_slot(slot, carry):
        row = pos_ref[2 * slot] + RIM
        col = pos_ref[2 * slot + 1] + RIM
        col_ids = lax.broadcasted_iota(jnp.int32, (step, SIDE), 1)
        row_ids = lax.broadcasted_iota(jnp.int32, (step, SIDE), 0)
        here_col = col_ids >= col
        for rows in blocks:
            here_row = row_ids >= row - rows.start
            far_rows = slice(rows.start + SIDE, rows.stop + SIDE)
            for c in range(2):
                first = jnp.where(here_row, ext_ref[c, rows, 0:SIDE], ext_ref[c, far_rows, 0:SIDE])
                second = jnp.where(here_row, ext_ref[c, rows, SIDE:], ext_ref[c, far_rows, SIDE:])
                window_ref[c, rows] = jnp.where(here_col, first, second)
                turned = rows_from(twice_ref, c, SIDE - row, rows.start)
                shifted_ref[c, rows] = pltpu.roll(turned, col, 1)
            pr, pi = shifted_ref[0, rows], shifted_ref[1, rows]
            wr, wi = window_ref[0, rows], window_ref[1, rows]
            put(rows, pr * wr - pi * wi, pr * wi + pi * wr)
        mid_ref[...] = dot(left_fwd_ref[...], stack_ref[...])
        for rows in blocks:
            far = dot(wide(mid_ref[rows]), right_fwd_ref[...])
            far_real, far_imag = far[:, 0:SIDE], far[:, SIDE:]
            misfit = far_real * far_real + far_imag * far_imag - intensity_ref[slot, rows]
            bent = jnp.concatenate([misfit * far_real, misfit * far_imag], axis=1)
            turned = dot(wide(bent), right_inv_ref[...])
            put(rows, turned[:, 0:SIDE], turned[:, SIDE:])
        mid_ref[...] = dot(left_inv_ref[...], stack_ref[...])
        for rows in blocks:
            here_row = row_ids >= row - rows.start
            far_rows = slice(rows.start + SIDE, rows.stop + SIDE)
            br, bi = mid_ref[rows, 0:SIDE], mid_ref[rows, SIDE:]
            pr, pi = shifted_ref[0, rows], shifted_ref[1, rows]
            wr, wi = window_ref[0, rows], window_ref[1, rows]
            for c, grad in enumerate((pr * br + pi * bi, pr * bi - pi * br)):
                first = jnp.where(here_col, grad, 0.0)
                second = jnp.where(here_col, 0.0, grad)
                for piece, cols in ((first, slice(0, SIDE)), (second, slice(SIDE, WIDE))):
                    near = jnp.where(here_row, piece, 0.0)
                    away = jnp.where(here_row, 0.0, piece)
                    if rows.start < RIM:
                        gtop_ref[c, rows, cols] += near
                        gmid_ref[c, rows.start + RIM : rows.stop + RIM, cols] += away
                    else:
                        gmid_ref[c, rows.start - RIM : rows.stop - RIM, cols] += near
                        gbot_ref[c, rows.start - RIM : rows.stop - RIM, cols] += away
            for c, grad in enumerate((wr * br + wi * bi, wr * bi - wi * br)):
                back_ref[c, rows] = grad
                back_ref[c, far_rows] = grad
        for rows in blocks:
            for c in range(2):
                turned = rows_from(back_ref, c, row, rows.start)
                gprobe_ref[c, rows] += pltpu.roll(turned, (SIDE - col) & (SIDE - 1), 1)
        return carry

    lax.fori_loop(0, counts_ref[0], one_slot, 0)


def all_slots(counts, positions, *arrays):
    smem = pl.BlockSpec(memory_space=pltpu.SMEM)
    vmem = pl.BlockSpec(memory_space=pltpu.VMEM)
    return pl.pallas_call(
        slots_kernel,
        out_shape=[
            jax.ShapeDtypeStruct((2, SIDE, SIDE), F32),
            jax.ShapeDtypeStruct((2, RIM, WIDE), F32),
            jax.ShapeDtypeStruct((2, RIM, WIDE), F32),
            jax.ShapeDtypeStruct((2, SIDE, WIDE), F32),
        ],
        in_specs=[smem, smem] + [vmem] * len(arrays),
        out_specs=[vmem] * 4,
        scratch_shapes=[
            pltpu.VMEM((2, WIDE, WIDE), F32),
            pltpu.VMEM((2, WIDE + 8, SIDE), F32),
            pltpu.VMEM((2, SIDE, SIDE), F32),
            pltpu.VMEM((2, SIDE, SIDE), F32),
            pltpu.VMEM((3 * WIDE, WIDE), BF16),
            pltpu.VMEM((SIDE, WIDE), F32),
            pltpu.VMEM((2, WIDE + 8, SIDE), F32),
        ],
        compiler_params=pltpu.CompilerParams(vmem_limit_bytes=32 * 1024 * 1024),
        cost_estimate=pl.CostEstimate(flops=10_000_000_000, bytes_accessed=20_000_000, transcendentals=0),
    )(counts, positions, *arrays)


def shifted(block, axes, distance):
    count = lax.axis_size(axes)
    route = [(i, i + distance) for i in range(count) if 0 <= i + distance < count]
    return lax.ppermute(block, axes, route)


def swap(pieces, axes):
    return lax.all_to_all(pieces, axes, split_axis=0, concat_axis=0, tiled=True)


def spread(block, axes):
    count = lax.axis_size(axes)
    return swap(jnp.broadcast_to(block[None], (count,) + block.shape), axes)


def summed_everywhere(grad):
    count = lax.axis_size(PLANE)
    pieces = swap(grad.reshape(count, 2 * SIDE // count, SIDE), PLANE)
    part = spread(jnp.sum(pieces, axis=0), DEEP)
    whole = spread(jnp.sum(part, axis=0), PLANE)
    return whole.reshape(2, SIDE, SIDE)


def shards(object_field, probe_field, intensity, positions, counts):
    tables = [jnp.asarray(t) for t in spectral_tables()]
    side_l = shifted(object_field[:, :, RIM:], COL, 1)
    side_r = shifted(object_field[:, :, :RIM], COL, -1)
    top = shifted(object_field[:, RIM:], ROW, 1)
    bottom = shifted(object_field[:, :RIM], ROW, -1)
    sides = jnp.concatenate([side_l, side_r], axis=2)
    corner_top = shifted(sides[:, RIM:], ROW, 1)
    corner_bottom = shifted(sides[:, :RIM], ROW, -1)
    grad_probe, grad_top, grad_bottom, grad_mid = all_slots(
        counts.reshape(1),
        positions.reshape(-1),
        object_field,
        side_l,
        side_r,
        top,
        bottom,
        corner_top,
        corner_bottom,
        probe_field,
        intensity[0, 0],
        *tables,
    )
    from_above = shifted(grad_bottom, ROW, 1)
    from_below = shifted(grad_top, ROW, -1)
    probe_gradient = summed_everywhere(grad_probe)
    rows = grad_mid + jnp.concatenate([from_above, from_below], axis=1)
    from_left = shifted(rows[:, :, RIM + SIDE :], COL, 1)
    from_right = shifted(rows[:, :, :RIM], COL, -1)
    gathered = rows[:, :, RIM : RIM + SIDE] + jnp.concatenate([from_left, from_right], axis=2)
    total_slots = lax.axis_size(ROW) * lax.axis_size(COL) * positions.shape[2]
    probe_update = probe_gradient * (1.0 / math.sqrt(total_slots))
    object_new = object_field - OBJECT_RATE * gathered
    return (object_new, probe_update)


def solution(mesh):
    chips = Mesh(mesh.devices.reshape(2, 4, 2, 16, 2), ("yh", "x", "core", "z", "yl"))
    placed = (
        P(None, ROW, COL),
        P(),
        P(ROW, COL, None, None, None),
        P(ROW, COL, None, None),
        P(ROW, COL),
    )
    return jax.shard_map(
        shards, mesh=chips, in_specs=placed, out_specs=(P(None, ROW, COL), P()), check_vma=False
    )
```

```python
import math

import jax
import jax.numpy as jnp
import ml_dtypes
import numpy as np
from jax import lax
from jax.experimental import pallas as pl
from jax.experimental.pallas import tpu as pltpu
from jax.sharding import Mesh, PartitionSpec as P

OBJECT_RATE = 0.5
ROW = ("yh", "x", "core")
COL = ("z", "yl")
PLANE = ("yh", "x", "core", "yl")
DEEP = "z"
SIDE = 256
RIM = 128
WIDE = 2 * SIDE
F32 = jnp.float32
BF16 = jnp.bfloat16


def two_terms(table):
    high = table.astype(np.float32).astype(ml_dtypes.bfloat16)
    low = (table - high.astype(np.float64)).astype(np.float32).astype(ml_dtypes.bfloat16)
    return high, low


def spectral_tables():
    index = np.arange(SIDE)
    angles = (index[:, None] * index[None, :] % SIDE) * (2.0 * math.pi / SIDE)
    cos, sin = np.cos(angles) / 16.0, np.sin(angles) / 16.0
    left = np.concatenate(two_terms(np.concatenate([cos, sin], 1)), 1)
    right = np.concatenate(two_terms(np.block([[cos, -sin], [sin, cos]])), 0)
    return left, right


def split(value):
    high = value.astype(BF16)
    low = (value - high.astype(F32)).astype(BF16)
    return high, low


UNROLL = 3
STEP = 64
BLOCKS = [slice(k, k + STEP) for k in range(0, SIDE, STEP)]
VMEM_BYTES = 62 * 1024 * 1024


def slots_kernel(
    counts_ref, pos_ref, tile_ref, side_l_ref, side_r_ref, top_ref, bot_ref, ctop_ref, cbot_ref,
    probe_ref, intensity_ref, left_ref, right_ref,
    gprobe_out, gtop_out, gbot_out, gmid_out,
    ext_ref, over_ref, held_ref, leftv_ref, rightv_ref, shifted_ref, window_ref, stack_ref, rows_ref,
    mid_ref, far_ref, back_ref, grad_ref, gprobe_ref, sems, pattern_sems,
):
    dot = lambda a, b: jnp.dot(a, b, preferred_element_type=F32)
    low, own, high = slice(0, RIM), slice(RIM, RIM + SIDE), slice(RIM + SIDE, WIDE)
    moves = [
        (probe_ref, over_ref.at[:, 8 : 8 + SIDE]),
        (probe_ref.at[:, SIDE - 8 : SIDE], over_ref.at[:, 0:8]),
        (tile_ref, ext_ref.at[:, own, own]),
        (side_l_ref, ext_ref.at[:, own, low]),
        (side_r_ref, ext_ref.at[:, own, high]),
        (top_ref, ext_ref.at[:, low, own]),
        (bot_ref, ext_ref.at[:, high, own]),
        (ctop_ref.at[:, :, low], ext_ref.at[:, low, low]),
        (ctop_ref.at[:, :, RIM:SIDE], ext_ref.at[:, low, high]),
        (cbot_ref.at[:, :, low], ext_ref.at[:, high, low]),
        (cbot_ref.at[:, :, RIM:SIDE], ext_ref.at[:, high, high]),
        (left_ref, leftv_ref),
        (right_ref, rightv_ref),
    ]
    copies = [pltpu.make_async_copy(src, dst, sems.at[k]) for k, (src, dst) in enumerate(moves)]
    groups = (counts_ref[0] + UNROLL - 1) // UNROLL

    def patterns(group):
        some = pl.ds(group * UNROLL, UNROLL)
        return pltpu.make_async_copy(intensity_ref.at[some], held_ref.at[some], pattern_sems.at[group])

    for copy in copies:
        copy.start()
    lax.fori_loop(0, groups, lambda group, carry: (patterns(group).start(), carry)[1], 0)
    gprobe_ref[...] = jnp.zeros((2, SIDE, SIDE), F32)
    grad_ref[...] = jnp.zeros((2, WIDE, WIDE), F32)
    for copy in copies[:-2]:
        copy.wait()

    def put(u, rows, real, imag):
        real_high, real_low = split(real)
        imag_high, imag_low = split(imag)
        for base, re, im in ((0, real_high, imag_high), (WIDE, real_low, imag_low)):
            upper = slice(base + rows.start, base + rows.stop)
            lower = slice(base + SIDE + rows.start, base + SIDE + rows.stop)
            stack_ref[u, upper, 0:SIDE] = re
            stack_ref[u, upper, SIDE:] = im
            stack_ref[u, lower, 0:SIDE] = im
            stack_ref[u, lower, SIDE:] = -re

    def put_rows(u, rows, real, imag):
        for base, part in ((0, real), (SIDE, imag)):
            high_part, low_part = split(part)
            rows_ref[u, rows, base : base + SIDE] = high_part
            rows_ref[u, rows, WIDE + base : WIDE + base + SIDE] = low_part

    def by_rows(u):
        lh, ll = leftv_ref[:, 0:WIDE], leftv_ref[:, WIDE:]
        xh, xl = stack_ref[u, 0:WIDE], stack_ref[u, WIDE:]
        return dot(lh, xh) + (dot(lh, xl) + dot(ll, xh))

    def by_cols(u):
        xh, xl = rows_ref[u, :, 0:WIDE], rows_ref[u, :, WIDE:]
        rh, rl = rightv_ref[0:WIDE], rightv_ref[WIDE:]
        return dot(xh, rh) + (dot(xl, rh) + dot(xh, rl))

    def one_group(group, carry):
        lanes = lambda n: lax.broadcasted_iota(jnp.int32, (n, RIM), 1)
        first_rows = lax.broadcasted_iota(jnp.int32, (8, RIM), 0)
        slots = [group * UNROLL + u for u in range(UNROLL)]
        alive = [s < counts_ref[0] for s in slots]
        live = [jnp.where(a, 1.0, 0.0).astype(F32) for a in alive]
        row = [jnp.where(a, pos_ref[2 * s], 0) + RIM for s, a in zip(slots, alive)]
        col = [jnp.where(a, pos_ref[2 * s + 1], 0) + RIM for s, a in zip(slots, alive)]
        down = [r & 7 for r in row]
        right = [c & (RIM - 1) for c in col]
        row = [pl.multiple_of(r - d, 8) for r, d in zip(row, down)]
        col = [pl.multiple_of(c - d, RIM) for c, d in zip(col, right)]
        strips = [[pl.ds(pl.multiple_of(c + k * RIM, RIM), RIM) for k in range(3)] for c in col]
        pieces = [(0, 8)] + [(8, STEP - 8)] + [(k, STEP) for k in range(STEP, SIDE, STEP)]

        def at(u, start, count):
            return pl.ds(pl.multiple_of(row[u] + start, 8), count)

        for u in range(UNROLL):
            for start, count in pieces:
                rows = slice(start, start + count)
                for c in range(2):
                    three = [ext_ref[c, at(u, start, count), strip] for strip in strips[u]]
                    if start == 0:
                        wrapped = [ext_ref[c, at(u, SIDE, 8), strip] for strip in strips[u]]
                        three = [jnp.where(first_rows >= down[u], a, b) for a, b in zip(three, wrapped)]
                    window_ref[u, c, rows, 0:RIM] = jnp.where(lanes(count) >= right[u], three[0], three[2])
                    window_ref[u, c, rows, RIM:] = three[1]
            for rows in BLOCKS:
                for c in range(2):
                    turned = pltpu.roll(over_ref[c, rows.start : rows.stop + 8], STEP + down[u], 0)[0:STEP]
                    shifted_ref[u, c, rows] = pltpu.roll(turned, right[u], 1)
                pr, pi = shifted_ref[u, 0, rows], shifted_ref[u, 1, rows]
                wr, wi = window_ref[u, 0, rows], window_ref[u, 1, rows]
                put(u, rows, pr * wr - pi * wi, pr * wi + pi * wr)
            mid_ref[u] = by_rows(u)
        for u in range(UNROLL):
            for rows in BLOCKS:
                put_rows(u, rows, mid_ref[u, rows, 0:SIDE], mid_ref[u, rows, SIDE:])
            far_ref[u] = by_cols(u)
        patterns(group).wait()
        for u in range(UNROLL):
            for rows in BLOCKS:
                far_real, far_imag = far_ref[u, rows, 0:SIDE], far_ref[u, rows, SIDE:]
                misfit = far_real * far_real + far_imag * far_imag - held_ref[slots[u], rows]
                misfit = misfit * live[u]
                put_rows(u, rows, misfit * far_real, -misfit * far_imag)
            mid_ref[u] = by_cols(u)
        for u in range(UNROLL):
            for rows in BLOCKS:
                put(u, rows, mid_ref[u, rows, 0:SIDE], mid_ref[u, rows, SIDE:])
            mid_ref[u] = by_rows(u)
        for u in range(UNROLL):
            for start, count in pieces:
                rows = slice(start, start + count)
                br, bi = mid_ref[u, rows, 0:SIDE], -mid_ref[u, rows, SIDE:]
                pr, pi = shifted_ref[u, 0, rows], shifted_ref[u, 1, rows]
                wr, wi = window_ref[u, 0, rows], window_ref[u, 1, rows]
                here = lanes(count) >= right[u]
                for c, grad in enumerate((pr * br + pi * bi, pr * bi - pi * br)):
                    left_part = grad[:, 0:RIM]
                    three = [jnp.where(here, left_part, 0.0), grad[:, RIM:], jnp.where(here, 0.0, left_part)]
                    for part, strip in zip(three, strips[u]):
                        if start == 0:
                            near = first_rows >= down[u]
                            grad_ref[c, at(u, SIDE, 8), strip] += jnp.where(near, 0.0, part)
                            part = jnp.where(near, part, 0.0)
                        grad_ref[c, at(u, start, count), strip] += part
                for c, grad in enumerate((wr * br + wi * bi, wr * bi - wi * br)):
                    back_ref[u, c, rows] = grad
                    if start == 0:
                        back_ref[u, c, SIDE : SIDE + 8] = grad
            for rows in BLOCKS:
                for c in range(2):
                    back = jnp.where(down[u] == 0, 0, STEP + 8 - down[u])
                    turned = pltpu.roll(back_ref[u, c, rows.start : rows.stop + 8], back, 0)[0:STEP]
                    gprobe_ref[c, rows] += pltpu.roll(turned, (SIDE - right[u]) & (SIDE - 1), 1)
        return carry

    for copy in copies[-2:]:
        copy.wait()
    lax.fori_loop(0, groups, one_group, 0)
    moves = [
        (gprobe_ref, gprobe_out),
        (grad_ref.at[:, low], gtop_out),
        (grad_ref.at[:, high], gbot_out),
        (grad_ref.at[:, own], gmid_out),
    ]
    copies = [pltpu.make_async_copy(src, dst, sems.at[k]) for k, (src, dst) in enumerate(moves)]
    for copy in copies:
        copy.start()
    for copy in copies:
        copy.wait()


def all_slots(counts, positions, *arrays):
    smem = pl.BlockSpec(memory_space=pltpu.SMEM)
    anywhere = pl.BlockSpec(memory_space=pl.ANY)
    return pl.pallas_call(
        slots_kernel,
        out_shape=[
            jax.ShapeDtypeStruct((2, SIDE, SIDE), F32),
            jax.ShapeDtypeStruct((2, RIM, WIDE), F32),
            jax.ShapeDtypeStruct((2, RIM, WIDE), F32),
            jax.ShapeDtypeStruct((2, SIDE, WIDE), F32),
        ],
        in_specs=[smem, smem] + [anywhere] * len(arrays),
        out_specs=[anywhere] * 4,
        scratch_shapes=[
            pltpu.VMEM((2, WIDE, WIDE), F32),
            pltpu.VMEM((2, SIDE + 8, SIDE), F32),
            pltpu.VMEM((6, SIDE, SIDE), F32),
            pltpu.VMEM((SIDE, 2 * WIDE), BF16),
            pltpu.VMEM((2 * WIDE, WIDE), BF16),
            pltpu.VMEM((UNROLL, 2, SIDE, SIDE), F32),
            pltpu.VMEM((UNROLL, 2, SIDE, SIDE), F32),
            pltpu.VMEM((UNROLL, 2 * WIDE, WIDE), BF16),
            pltpu.VMEM((UNROLL, SIDE, 2 * WIDE), BF16),
            pltpu.VMEM((UNROLL, SIDE, WIDE), F32),
            pltpu.VMEM((UNROLL, SIDE, WIDE), F32),
            pltpu.VMEM((UNROLL, 2, SIDE + 8, SIDE), F32),
            pltpu.VMEM((2, WIDE, WIDE), F32),
            pltpu.VMEM((2, SIDE, SIDE), F32),
            pltpu.SemaphoreType.DMA((13,)),
            pltpu.SemaphoreType.DMA((6 // UNROLL,)),
        ],
        compiler_params=pltpu.CompilerParams(vmem_limit_bytes=VMEM_BYTES),
        cost_estimate=pl.CostEstimate(flops=10_000_000_000, bytes_accessed=20_000_000, transcendentals=0),
    )(counts, positions, *arrays)


def shifted(block, axes, distance):
    count = lax.axis_size(axes)
    route = [(i, i + distance) for i in range(count) if 0 <= i + distance < count]
    return lax.ppermute(block, axes, route)


def swap(pieces, axes):
    return lax.all_to_all(pieces, axes, split_axis=0, concat_axis=0, tiled=True)


def spread(block, axes):
    count = lax.axis_size(axes)
    return swap(jnp.broadcast_to(block[None], (count,) + block.shape), axes)


def summed_everywhere(grad):
    count = lax.axis_size(PLANE)
    pieces = swap(grad.reshape(count, 2 * SIDE // count, SIDE), PLANE)
    part = spread(jnp.sum(pieces, axis=0), DEEP)
    whole = spread(jnp.sum(part, axis=0), PLANE)
    return whole.reshape(2, SIDE, SIDE)


def shards(object_field, probe_field, intensity, positions, counts):
    tables = [jnp.asarray(t) for t in spectral_tables()]
    side_l = shifted(object_field[:, :, RIM:], COL, 1)
    side_r = shifted(object_field[:, :, :RIM], COL, -1)
    top = shifted(object_field[:, RIM:], ROW, 1)
    bottom = shifted(object_field[:, :RIM], ROW, -1)
    sides = jnp.concatenate([side_l, side_r], axis=2)
    corner_top = shifted(sides[:, RIM:], ROW, 1)
    corner_bottom = shifted(sides[:, :RIM], ROW, -1)
    grad_probe, grad_top, grad_bottom, grad_mid = all_slots(
        counts.reshape(1),
        positions.reshape(-1),
        object_field,
        side_l,
        side_r,
        top,
        bottom,
        corner_top,
        corner_bottom,
        probe_field,
        intensity[0, 0],
        *tables,
    )
    from_above = shifted(grad_bottom, ROW, 1)
    from_below = shifted(grad_top, ROW, -1)
    probe_gradient = summed_everywhere(grad_probe)
    rows = grad_mid + jnp.concatenate([from_above, from_below], axis=1)
    from_left = shifted(rows[:, :, RIM + SIDE :], COL, 1)
    from_right = shifted(rows[:, :, :RIM], COL, -1)
    gathered = rows[:, :, RIM : RIM + SIDE] + jnp.concatenate([from_left, from_right], axis=2)
    total_slots = lax.axis_size(ROW) * lax.axis_size(COL) * positions.shape[2]
    probe_update = probe_gradient * (1.0 / math.sqrt(total_slots))
    object_new = object_field - OBJECT_RATE * gathered
    return (object_new, probe_update)


def solution(mesh):
    chips = Mesh(mesh.devices.reshape(2, 4, 2, 16, 2), ("yh", "x", "core", "z", "yl"))
    placed = (
        P(None, ROW, COL),
        P(),
        P(ROW, COL, None, None, None),
        P(ROW, COL, None, None),
        P(ROW, COL),
    )
    return jax.shard_map(
        shards, mesh=chips, in_specs=placed, out_specs=(P(None, ROW, COL), P()), check_vma=False
    )
```

```python
import math

import jax
import jax.numpy as jnp
import ml_dtypes
import numpy as np
from jax import lax
from jax.experimental import pallas as pl
from jax.experimental.pallas import tpu as pltpu
from jax.sharding import Mesh, PartitionSpec as P

OBJECT_RATE = 0.5
ROW = ("yh", "x", "core")
COL = ("z", "yl")
PLANE = ("yh", "x", "core", "yl")
DEEP = "z"
SIDE = 256
RIM = 128
WIDE = 2 * SIDE
F32 = jnp.float32
BF16 = jnp.bfloat16


def two_terms(table):
    high = table.astype(np.float32).astype(ml_dtypes.bfloat16)
    low = (table - high.astype(np.float64)).astype(np.float32).astype(ml_dtypes.bfloat16)
    return high, low


def spectral_tables():
    index = np.arange(SIDE)
    angles = (index[:, None] * index[None, :] % SIDE) * (2.0 * math.pi / SIDE)
    cos, sin = np.cos(angles) / 16.0, np.sin(angles) / 16.0
    return (np.concatenate(two_terms(np.concatenate([cos, sin], 1)), 1),)


def split(value):
    high = value.astype(BF16)
    low = (value - high.astype(F32)).astype(BF16)
    return high, low


UNROLL = 3
STEP = 64
BLOCKS = [slice(k, k + STEP) for k in range(0, SIDE, STEP)]
VMEM_BYTES = 50 * 1024 * 1024


def slots_kernel(
    counts_ref, pos_ref, tile_ref, side_l_ref, side_r_ref, top_ref, bot_ref, probe_ref, intensity_ref, left_ref,
    gprobe_out, gtop_out, gbot_out, gmid_out,
    ext_ref, over_ref, held_ref, leftv_ref, rightv_ref, shifted_ref, window_ref, stack_ref, rows_ref,
    mid_ref, far_ref, back_ref, grad_ref, gprobe_ref, sems, pattern_sems,
):
    dot = lambda a, b: jnp.dot(a, b, preferred_element_type=F32)
    low, own, high = slice(0, RIM), slice(RIM, RIM + SIDE), slice(RIM + SIDE, WIDE)
    moves = [
        (probe_ref, over_ref.at[:, 8 : 8 + SIDE]),
        (probe_ref.at[:, SIDE - 8 : SIDE], over_ref.at[:, 0:8]),
        (tile_ref, ext_ref.at[:, own, own]),
        (side_l_ref, ext_ref.at[:, own, low]),
        (side_r_ref, ext_ref.at[:, own, high]),
        (left_ref, leftv_ref),
        (top_ref, ext_ref.at[:, low]),
        (bot_ref, ext_ref.at[:, high]),
    ]
    copies = [pltpu.make_async_copy(src, dst, sems.at[k]) for k, (src, dst) in enumerate(moves)]
    groups = (counts_ref[0] + UNROLL - 1) // UNROLL

    def patterns(group):
        some = pl.ds(group * UNROLL, UNROLL)
        return pltpu.make_async_copy(intensity_ref.at[some], held_ref.at[some], pattern_sems.at[group])

    for copy in copies:
        copy.start()
    lax.fori_loop(0, groups, lambda group, carry: (patterns(group).start(), carry)[1], 0)
    gprobe_ref[...] = jnp.zeros((2, SIDE, SIDE), F32)
    grad_ref[...] = jnp.zeros((2, WIDE, WIDE), F32)
    for copy in copies:
        copy.wait()
    for k in range(2):
        cos, sin = leftv_ref[:, k * WIDE : k * WIDE + SIDE], leftv_ref[:, k * WIDE + SIDE : (k + 1) * WIDE]
        rightv_ref[k * WIDE : k * WIDE + SIDE, 0:SIDE] = cos
        rightv_ref[k * WIDE : k * WIDE + SIDE, SIDE:] = -sin
        rightv_ref[k * WIDE + SIDE : (k + 1) * WIDE, 0:SIDE] = sin
        rightv_ref[k * WIDE + SIDE : (k + 1) * WIDE, SIDE:] = cos

    def put(u, rows, real, imag):
        real_high, real_low = split(real)
        imag_high, imag_low = split(imag)
        for base, re, im in ((0, real_high, imag_high), (WIDE, real_low, imag_low)):
            upper = slice(base + rows.start, base + rows.stop)
            lower = slice(base + SIDE + rows.start, base + SIDE + rows.stop)
            stack_ref[u, upper, 0:SIDE] = re
            stack_ref[u, upper, SIDE:] = im
            stack_ref[u, lower, 0:SIDE] = im
            stack_ref[u, lower, SIDE:] = -re

    def put_rows(u, rows, real, imag):
        for base, part in ((0, real), (SIDE, imag)):
            high_part, low_part = split(part)
            rows_ref[u, rows, base : base + SIDE] = high_part
            rows_ref[u, rows, WIDE + base : WIDE + base + SIDE] = low_part

    def by_rows(u):
        lh, ll = leftv_ref[:, 0:WIDE], leftv_ref[:, WIDE:]
        xh, xl = stack_ref[u, 0:WIDE], stack_ref[u, WIDE:]
        return dot(lh, xh) + (dot(lh, xl) + dot(ll, xh))

    def by_cols(u):
        xh, xl = rows_ref[u, :, 0:WIDE], rows_ref[u, :, WIDE:]
        rh, rl = rightv_ref[0:WIDE], rightv_ref[WIDE:]
        return dot(xh, rh) + (dot(xl, rh) + dot(xh, rl))

    def one_group(group, carry):
        lanes = lambda n: lax.broadcasted_iota(jnp.int32, (n, RIM), 1)
        first_rows = lax.broadcasted_iota(jnp.int32, (8, RIM), 0)
        slots = [group * UNROLL + u for u in range(UNROLL)]
        alive = [s < counts_ref[0] for s in slots]
        live = [jnp.where(a, 1.0, 0.0).astype(F32) for a in alive]
        row = [jnp.where(a, pos_ref[2 * s], 0) + RIM for s, a in zip(slots, alive)]
        col = [jnp.where(a, pos_ref[2 * s + 1], 0) + RIM for s, a in zip(slots, alive)]
        down = [r & 7 for r in row]
        right = [c & (RIM - 1) for c in col]
        row = [pl.multiple_of(r - d, 8) for r, d in zip(row, down)]
        col = [pl.multiple_of(c - d, RIM) for c, d in zip(col, right)]
        strips = [[pl.ds(pl.multiple_of(c + k * RIM, RIM), RIM) for k in range(3)] for c in col]
        pieces = [(0, 8)] + [(8, STEP - 8)] + [(k, STEP) for k in range(STEP, SIDE, STEP)]

        def at(u, start, count):
            return pl.ds(pl.multiple_of(row[u] + start, 8), count)

        for u in range(UNROLL):
            for start, count in pieces:
                rows = slice(start, start + count)
                for c in range(2):
                    three = [ext_ref[c, at(u, start, count), strip] for strip in strips[u]]
                    if start == 0:
                        wrapped = [ext_ref[c, at(u, SIDE, 8), strip] for strip in strips[u]]
                        three = [jnp.where(first_rows >= down[u], a, b) for a, b in zip(three, wrapped)]
                    window_ref[u, c, rows, 0:RIM] = jnp.where(lanes(count) >= right[u], three[0], three[2])
                    window_ref[u, c, rows, RIM:] = three[1]
            for rows in BLOCKS:
                for c in range(2):
                    turned = pltpu.roll(over_ref[c, rows.start : rows.stop + 8], STEP + down[u], 0)[0:STEP]
                    shifted_ref[u, c, rows] = pltpu.roll(turned, right[u], 1)
                pr, pi = shifted_ref[u, 0, rows], shifted_ref[u, 1, rows]
                wr, wi = window_ref[u, 0, rows], window_ref[u, 1, rows]
                put(u, rows, pr * wr - pi * wi, pr * wi + pi * wr)
            mid_ref[u] = by_rows(u)
        for u in range(UNROLL):
            for rows in BLOCKS:
                put_rows(u, rows, mid_ref[u, rows, 0:SIDE], mid_ref[u, rows, SIDE:])
            far_ref[u] = by_cols(u)
        patterns(group).wait()
        for u in range(UNROLL):
            for rows in BLOCKS:
                far_real, far_imag = far_ref[u, rows, 0:SIDE], far_ref[u, rows, SIDE:]
                misfit = far_real * far_real + far_imag * far_imag - held_ref[slots[u], rows]
                misfit = misfit * live[u]
                put_rows(u, rows, misfit * far_real, -misfit * far_imag)
            mid_ref[u] = by_cols(u)
        for u in range(UNROLL):
            for rows in BLOCKS:
                put(u, rows, mid_ref[u, rows, 0:SIDE], mid_ref[u, rows, SIDE:])
            mid_ref[u] = by_rows(u)
        for u in range(UNROLL):
            for start, count in pieces:
                rows = slice(start, start + count)
                br, bi = mid_ref[u, rows, 0:SIDE], -mid_ref[u, rows, SIDE:]
                pr, pi = shifted_ref[u, 0, rows], shifted_ref[u, 1, rows]
                wr, wi = window_ref[u, 0, rows], window_ref[u, 1, rows]
                here = lanes(count) >= right[u]
                for c, grad in enumerate((pr * br + pi * bi, pr * bi - pi * br)):
                    left_part = grad[:, 0:RIM]
                    three = [jnp.where(here, left_part, 0.0), grad[:, RIM:], jnp.where(here, 0.0, left_part)]
                    for part, strip in zip(three, strips[u]):
                        if start == 0:
                            near = first_rows >= down[u]
                            grad_ref[c, at(u, SIDE, 8), strip] += jnp.where(near, 0.0, part)
                            part = jnp.where(near, part, 0.0)
                        grad_ref[c, at(u, start, count), strip] += part
                for c, grad in enumerate((wr * br + wi * bi, wr * bi - wi * br)):
                    back_ref[u, c, rows] = grad
                    if start == 0:
                        back_ref[u, c, SIDE : SIDE + 8] = grad
            for rows in BLOCKS:
                for c in range(2):
                    back = jnp.where(down[u] == 0, 0, STEP + 8 - down[u])
                    turned = pltpu.roll(back_ref[u, c, rows.start : rows.stop + 8], back, 0)[0:STEP]
                    gprobe_ref[c, rows] += pltpu.roll(turned, (SIDE - right[u]) & (SIDE - 1), 1)
        return carry

    lax.fori_loop(0, groups, one_group, 0)
    moves = [
        (gprobe_ref, gprobe_out),
        (grad_ref.at[:, low], gtop_out),
        (grad_ref.at[:, high], gbot_out),
        (grad_ref.at[:, own], gmid_out),
    ]
    copies = [pltpu.make_async_copy(src, dst, sems.at[k]) for k, (src, dst) in enumerate(moves)]
    for copy in copies:
        copy.start()
    for copy in copies:
        copy.wait()


def all_slots(counts, positions, *arrays):
    smem = pl.BlockSpec(memory_space=pltpu.SMEM)
    anywhere = pl.BlockSpec(memory_space=pl.ANY)
    return pl.pallas_call(
        slots_kernel,
        out_shape=[
            jax.ShapeDtypeStruct((2, SIDE, SIDE), F32),
            jax.ShapeDtypeStruct((2, RIM, WIDE), F32),
            jax.ShapeDtypeStruct((2, RIM, WIDE), F32),
            jax.ShapeDtypeStruct((2, SIDE, WIDE), F32),
        ],
        in_specs=[smem, smem] + [anywhere] * len(arrays),
        out_specs=[anywhere] * 4,
        scratch_shapes=[
            pltpu.VMEM((2, WIDE, WIDE), F32),
            pltpu.VMEM((2, SIDE + 8, SIDE), F32),
            pltpu.VMEM((6, SIDE, SIDE), F32),
            pltpu.VMEM((SIDE, 2 * WIDE), BF16),
            pltpu.VMEM((2 * WIDE, WIDE), BF16),
            pltpu.VMEM((UNROLL, 2, SIDE, SIDE), F32),
            pltpu.VMEM((UNROLL, 2, SIDE, SIDE), F32),
            pltpu.VMEM((UNROLL, 2 * WIDE, WIDE), BF16),
            pltpu.VMEM((UNROLL, SIDE, 2 * WIDE), BF16),
            pltpu.VMEM((UNROLL, SIDE, WIDE), F32),
            pltpu.VMEM((UNROLL, SIDE, WIDE), F32),
            pltpu.VMEM((UNROLL, 2, SIDE + 8, SIDE), F32),
            pltpu.VMEM((2, WIDE, WIDE), F32),
            pltpu.VMEM((2, SIDE, SIDE), F32),
            pltpu.SemaphoreType.DMA((8,)),
            pltpu.SemaphoreType.DMA((6 // UNROLL,)),
        ],
        compiler_params=pltpu.CompilerParams(vmem_limit_bytes=VMEM_BYTES),
        cost_estimate=pl.CostEstimate(flops=10_000_000_000, bytes_accessed=20_000_000, transcendentals=0),
    )(counts, positions, *arrays)


def shifted(block, axes, distance):
    count = lax.axis_size(axes)
    route = [(i, i + distance) for i in range(count) if 0 <= i + distance < count]
    return lax.ppermute(block, axes, route)


def swap(pieces, axes):
    return lax.all_to_all(pieces, axes, split_axis=0, concat_axis=0, tiled=True)


def spread(block, axes):
    count = lax.axis_size(axes)
    return swap(jnp.broadcast_to(block[None], (count,) + block.shape), axes)


def summed_everywhere(grad, scale):
    count = lax.axis_size(PLANE)
    pieces = swap(grad.reshape(count, 2 * SIDE // count, SIDE), PLANE)
    part = spread(jnp.sum(pieces, axis=0), DEEP)
    whole = spread(jnp.sum(part, axis=0) * scale, PLANE)
    return whole.reshape(2, SIDE, SIDE)


def shards(object_field, probe_field, intensity, positions, counts):
    tables = [jnp.asarray(t) for t in spectral_tables()]
    side_l = shifted(object_field[:, :, RIM:], COL, 1)
    side_r = shifted(object_field[:, :, :RIM], COL, -1)
    middle = jnp.concatenate([side_l, object_field, side_r], axis=2)
    top = shifted(middle[:, RIM:], ROW, 1)
    bottom = shifted(middle[:, :RIM], ROW, -1)
    grad_probe, grad_top, grad_bottom, grad_mid = all_slots(
        counts.reshape(1),
        positions.reshape(-1),
        object_field,
        side_l,
        side_r,
        top,
        bottom,
        probe_field,
        intensity[0, 0],
        *tables,
    )
    from_above = shifted(grad_bottom, ROW, 1)
    from_below = shifted(grad_top, ROW, -1)
    total_slots = lax.axis_size(ROW) * lax.axis_size(COL) * positions.shape[2]
    probe_update = summed_everywhere(grad_probe, 1.0 / math.sqrt(total_slots))
    rows = grad_mid + jnp.concatenate([from_above, from_below], axis=1)
    from_left = shifted(rows[:, :, RIM + SIDE :], COL, 1)
    from_right = shifted(rows[:, :, :RIM], COL, -1)
    gathered = rows[:, :, RIM : RIM + SIDE] + jnp.concatenate([from_left, from_right], axis=2)
    object_new = object_field - OBJECT_RATE * gathered
    return (object_new, probe_update)


def solution(mesh):
    chips = Mesh(mesh.devices.reshape(2, 4, 2, 16, 2), ("yh", "x", "core", "z", "yl"))
    placed = (
        P(None, ROW, COL),
        P(),
        P(ROW, COL, None, None, None),
        P(ROW, COL, None, None),
        P(ROW, COL),
    )
    return jax.shard_map(
        shards, mesh=chips, in_specs=placed, out_specs=(P(None, ROW, COL), P()), check_vma=False
    )
```

```python
import math

import jax
import jax.numpy as jnp
import ml_dtypes
import numpy as np
from jax import lax
from jax.experimental import pallas as pl
from jax.experimental.pallas import tpu as pltpu
from jax.sharding import Mesh, PartitionSpec as P

OBJECT_RATE = 0.5
ROW = ("yh", "x", "core")
COL = ("z", "yl")
PLANE = ("yh", "x", "core", "yl")
DEEP = "z"
SIDE = 256
RIM = 128
WIDE = 2 * SIDE
F32 = jnp.float32
BF16 = jnp.bfloat16


def two_terms(table):
    high = table.astype(np.float32).astype(ml_dtypes.bfloat16)
    low = (table - high.astype(np.float64)).astype(np.float32).astype(ml_dtypes.bfloat16)
    return high, low


def spectral_tables():
    index = np.arange(SIDE)
    angles = (index[:, None] * index[None, :] % SIDE) * (2.0 * math.pi / SIDE)
    cos, sin = np.cos(angles) / 16.0, np.sin(angles) / 16.0
    high, low = two_terms(np.stack([cos, -sin - cos, cos - sin]))
    return (np.stack([high, low]),)


def split(value):
    high = value.astype(BF16)
    low = (value - high.astype(F32)).astype(BF16)
    return high, low


UNROLL = 3
STEP = 64
BLOCKS = [slice(k, k + STEP) for k in range(0, SIDE, STEP)]
VMEM_BYTES = 50 * 1024 * 1024


def slots_kernel(
    counts_ref, pos_ref, tile_ref, side_l_ref, side_r_ref, top_ref, bot_ref, probe_ref, intensity_ref, tables_ref,
    gprobe_out, grad_ref,
    ext_ref, over_ref, held_ref, table_ref, shifted_ref, window_ref, terms_ref,
    mid_ref, far_ref, back_ref, gprobe_ref, sems, pattern_sems,
):
    dot = lambda a, b: jnp.dot(a, b, preferred_element_type=F32)
    low, own, high = slice(0, RIM), slice(RIM, RIM + SIDE), slice(RIM + SIDE, WIDE)
    moves = [
        (probe_ref, over_ref.at[:, 8 : 8 + SIDE]),
        (probe_ref.at[:, SIDE - 8 : SIDE], over_ref.at[:, 0:8]),
        (tile_ref, ext_ref.at[:, own, own]),
        (side_l_ref, ext_ref.at[:, own, low]),
        (side_r_ref, ext_ref.at[:, own, high]),
        (tables_ref, table_ref),
        (top_ref, ext_ref.at[:, low]),
        (bot_ref, ext_ref.at[:, high]),
    ]
    copies = [pltpu.make_async_copy(src, dst, sems.at[k]) for k, (src, dst) in enumerate(moves)]
    groups = (counts_ref[0] + UNROLL - 1) // UNROLL

    def patterns(group):
        some = pl.ds(group * UNROLL, UNROLL)
        return pltpu.make_async_copy(intensity_ref.at[some], held_ref.at[some], pattern_sems.at[group])

    for copy in copies:
        copy.start()
    lax.fori_loop(0, groups, lambda group, carry: (patterns(group).start(), carry)[1], 0)
    gprobe_ref[...] = jnp.zeros((2, SIDE, SIDE), F32)
    grad_ref[...] = jnp.zeros((2, WIDE, WIDE), F32)
    for copy in copies:
        copy.wait()

    def put(u, rows, real, imag):
        for k, part in enumerate((real + imag, real, imag)):
            terms_ref[u, 0, k, rows], terms_ref[u, 1, k, rows] = split(part)

    def three(u, left, product):
        both, first, second = (
            product(terms_ref[u, 0, k], table_ref[0, k])
            + (product(terms_ref[u, 1, k], table_ref[0, k]) + product(terms_ref[u, 0, k], table_ref[1, k]))
            for k in range(3)
        )
        left[u, :, 0:SIDE] = both - second
        left[u, :, SIDE:] = both + first

    def by_rows(u, left):
        three(u, left, lambda value, table: dot(table, value))

    def by_cols(u, left):
        three(u, left, dot)

    def one_group(group, carry):
        lanes = lambda n: lax.broadcasted_iota(jnp.int32, (n, RIM), 1)
        first_rows = lax.broadcasted_iota(jnp.int32, (8, RIM), 0)
        slots = [group * UNROLL + u for u in range(UNROLL)]
        alive = [s < counts_ref[0] for s in slots]
        live = [jnp.where(a, 1.0, 0.0).astype(F32) for a in alive]
        row = [jnp.where(a, pos_ref[2 * s], 0) + RIM for s, a in zip(slots, alive)]
        col = [jnp.where(a, pos_ref[2 * s + 1], 0) + RIM for s, a in zip(slots, alive)]
        down = [r & 7 for r in row]
        right = [c & (RIM - 1) for c in col]
        row = [pl.multiple_of(r - d, 8) for r, d in zip(row, down)]
        col = [pl.multiple_of(c - d, RIM) for c, d in zip(col, right)]
        strips = [[pl.ds(pl.multiple_of(c + k * RIM, RIM), RIM) for k in range(3)] for c in col]
        pieces = [(0, 8)] + [(8, STEP - 8)] + [(k, STEP) for k in range(STEP, SIDE, STEP)]

        def at(u, start, count):
            return pl.ds(pl.multiple_of(row[u] + start, 8), count)

        for u in range(UNROLL):
            for start, count in pieces:
                rows = slice(start, start + count)
                for c in range(2):
                    three = [ext_ref[c, at(u, start, count), strip] for strip in strips[u]]
                    if start == 0:
                        wrapped = [ext_ref[c, at(u, SIDE, 8), strip] for strip in strips[u]]
                        three = [jnp.where(first_rows >= down[u], a, b) for a, b in zip(three, wrapped)]
                    window_ref[u, c, rows, 0:RIM] = jnp.where(lanes(count) >= right[u], three[0], three[2])
                    window_ref[u, c, rows, RIM:] = three[1]
            for rows in BLOCKS:
                for c in range(2):
                    turned = pltpu.roll(over_ref[c, rows.start : rows.stop + 8], STEP + down[u], 0)[0:STEP]
                    shifted_ref[u, c, rows] = pltpu.roll(turned, right[u], 1)
                pr, pi = shifted_ref[u, 0, rows], shifted_ref[u, 1, rows]
                wr, wi = window_ref[u, 0, rows], window_ref[u, 1, rows]
                put(u, rows, pr * wr - pi * wi, pr * wi + pi * wr)
            by_rows(u, mid_ref)
        for u in range(UNROLL):
            for rows in BLOCKS:
                put(u, rows, mid_ref[u, rows, 0:SIDE], mid_ref[u, rows, SIDE:])
            by_cols(u, far_ref)
        patterns(group).wait()
        for u in range(UNROLL):
            for rows in BLOCKS:
                far_real, far_imag = far_ref[u, rows, 0:SIDE], far_ref[u, rows, SIDE:]
                misfit = far_real * far_real + far_imag * far_imag - held_ref[slots[u], rows]
                misfit = misfit * live[u]
                put(u, rows, misfit * far_real, -misfit * far_imag)
            by_cols(u, mid_ref)
        for u in range(UNROLL):
            for rows in BLOCKS:
                put(u, rows, mid_ref[u, rows, 0:SIDE], mid_ref[u, rows, SIDE:])
            by_rows(u, mid_ref)
        for u in range(UNROLL):
            for start, count in pieces:
                rows = slice(start, start + count)
                br, bi = mid_ref[u, rows, 0:SIDE], -mid_ref[u, rows, SIDE:]
                pr, pi = shifted_ref[u, 0, rows], shifted_ref[u, 1, rows]
                wr, wi = window_ref[u, 0, rows], window_ref[u, 1, rows]
                here = lanes(count) >= right[u]
                for c, grad in enumerate((pr * br + pi * bi, pr * bi - pi * br)):
                    left_part = grad[:, 0:RIM]
                    three = [jnp.where(here, left_part, 0.0), grad[:, RIM:], jnp.where(here, 0.0, left_part)]
                    for part, strip in zip(three, strips[u]):
                        if start == 0:
                            near = first_rows >= down[u]
                            grad_ref[c, at(u, SIDE, 8), strip] += jnp.where(near, 0.0, part)
                            part = jnp.where(near, part, 0.0)
                        grad_ref[c, at(u, start, count), strip] += part
                for c, grad in enumerate((wr * br + wi * bi, wr * bi - wi * br)):
                    back_ref[u, c, rows] = grad
                    if start == 0:
                        back_ref[u, c, SIDE : SIDE + 8] = grad
            for rows in BLOCKS:
                for c in range(2):
                    back = jnp.where(down[u] == 0, 0, STEP + 8 - down[u])
                    turned = pltpu.roll(back_ref[u, c, rows.start : rows.stop + 8], back, 0)[0:STEP]
                    gprobe_ref[c, rows] += pltpu.roll(turned, (SIDE - right[u]) & (SIDE - 1), 1)
        return carry

    lax.fori_loop(0, groups, one_group, 0)
    copy = pltpu.make_async_copy(gprobe_ref, gprobe_out, sems.at[0])
    copy.start()
    copy.wait()


def all_slots(counts, positions, *arrays):
    smem = pl.BlockSpec(memory_space=pltpu.SMEM)
    anywhere = pl.BlockSpec(memory_space=pl.ANY)
    return pl.pallas_call(
        slots_kernel,
        out_shape=[
            jax.ShapeDtypeStruct((2, SIDE, SIDE), F32),
            jax.ShapeDtypeStruct((2, WIDE, WIDE), F32),
        ],
        in_specs=[smem, smem] + [anywhere] * len(arrays),
        out_specs=[anywhere, pl.BlockSpec(memory_space=pltpu.VMEM)],
        scratch_shapes=[
            pltpu.VMEM((2, WIDE, WIDE), F32),
            pltpu.VMEM((2, SIDE + 8, SIDE), F32),
            pltpu.VMEM((6, SIDE, SIDE), F32),
            pltpu.VMEM((2, 3, SIDE, SIDE), BF16),
            pltpu.VMEM((UNROLL, 2, SIDE, SIDE), F32),
            pltpu.VMEM((UNROLL, 2, SIDE, SIDE), F32),
            pltpu.VMEM((UNROLL, 2, 3, SIDE, SIDE), BF16),
            pltpu.VMEM((UNROLL, SIDE, WIDE), F32),
            pltpu.VMEM((UNROLL, SIDE, WIDE), F32),
            pltpu.VMEM((UNROLL, 2, SIDE + 8, SIDE), F32),
            pltpu.VMEM((2, SIDE, SIDE), F32),
            pltpu.SemaphoreType.DMA((8,)),
            pltpu.SemaphoreType.DMA((6 // UNROLL,)),
        ],
        compiler_params=pltpu.CompilerParams(vmem_limit_bytes=VMEM_BYTES),
        cost_estimate=pl.CostEstimate(flops=10_000_000_000, bytes_accessed=20_000_000, transcendentals=0),
    )(counts, positions, *arrays)


def shifted(block, axes, distance):
    count = lax.axis_size(axes)
    route = [(i, i + distance) for i in range(count) if 0 <= i + distance < count]
    return lax.ppermute(block, axes, route)


def swap(pieces, axes):
    return lax.all_to_all(pieces, axes, split_axis=0, concat_axis=0, tiled=True)


def spread(block, axes):
    count = lax.axis_size(axes)
    return swap(jnp.broadcast_to(block[None], (count,) + block.shape), axes)


def summed_everywhere(grad, scale):
    count = lax.axis_size(PLANE)
    pieces = swap(grad.reshape(count, 2 * SIDE // count, SIDE), PLANE)
    part = spread(jnp.sum(pieces, axis=0), DEEP)
    whole = spread(jnp.sum(part, axis=0) * scale, PLANE)
    return whole.reshape(2, SIDE, SIDE)


def shards(object_field, probe_field, intensity, positions, counts):
    tables = [jnp.asarray(t) for t in spectral_tables()]
    side_l = shifted(object_field[:, :, RIM:], COL, 1)
    side_r = shifted(object_field[:, :, :RIM], COL, -1)
    middle = jnp.concatenate([side_l, object_field, side_r], axis=2)
    top = shifted(middle[:, RIM:], ROW, 1)
    bottom = shifted(middle[:, :RIM], ROW, -1)
    grad_probe, grad_wide = all_slots(
        counts.reshape(1),
        positions.reshape(-1),
        object_field,
        side_l,
        side_r,
        top,
        bottom,
        probe_field,
        intensity[0, 0],
        *tables,
    )
    from_above = shifted(grad_wide[:, RIM + SIDE :], ROW, 1)
    from_below = shifted(grad_wide[:, :RIM], ROW, -1)
    total_slots = lax.axis_size(ROW) * lax.axis_size(COL) * positions.shape[2]
    probe_update = summed_everywhere(grad_probe, 1.0 / math.sqrt(total_slots))
    rows = grad_wide[:, RIM : RIM + SIDE] + jnp.concatenate([from_above, from_below], axis=1)
    from_left = shifted(rows[:, :, RIM + SIDE :], COL, 1)
    from_right = shifted(rows[:, :, :RIM], COL, -1)
    gathered = rows[:, :, RIM : RIM + SIDE] + jnp.concatenate([from_left, from_right], axis=2)
    object_new = object_field - OBJECT_RATE * gathered
    return (object_new, probe_update)


def solution(mesh):
    chips = Mesh(mesh.devices.reshape(2, 4, 2, 16, 2), ("yh", "x", "core", "z", "yl"))
    placed = (
        P(None, ROW, COL),
        P(),
        P(ROW, COL, None, None, None),
        P(ROW, COL, None, None),
        P(ROW, COL),
    )
    return jax.shard_map(
        shards, mesh=chips, in_specs=placed, out_specs=(P(None, ROW, COL), P()), check_vma=False
    )
```

```python
import math

import jax
import jax.numpy as jnp
import ml_dtypes
import numpy as np
from jax import lax
from jax.experimental import pallas as pl
from jax.experimental.pallas import tpu as pltpu
from jax.sharding import Mesh, PartitionSpec as P

OBJECT_RATE = 0.5
ROW = ("yh", "x", "core")
COL = ("z", "yl")
PLANE = ("core", "yh", "x", "yl")
FLOOR = ("yh", "x", "yl")
DEEP = "z"
SIDE = 256
RIM = 128
WIDE = 2 * SIDE
F32 = jnp.float32
BF16 = jnp.bfloat16


def two_terms(table):
    high = table.astype(np.float32).astype(ml_dtypes.bfloat16)
    low = (table - high.astype(np.float64)).astype(np.float32).astype(ml_dtypes.bfloat16)
    return high, low


def spectral_tables():
    index = np.arange(SIDE)
    angles = (index[:, None] * index[None, :] % SIDE) * (2.0 * math.pi / SIDE)
    cos, sin = np.cos(angles) / 16.0, np.sin(angles) / 16.0
    high, low = two_terms(np.stack([cos, -sin - cos, cos - sin]))
    return (np.stack([high, low]),)


def split(value):
    high = value.astype(BF16)
    low = (value - high.astype(F32)).astype(BF16)
    return high, low


UNROLL = 3
STEP = 64
BLOCKS = [slice(k, k + STEP) for k in range(0, SIDE, STEP)]
VMEM_BYTES = 50 * 1024 * 1024


def slots_kernel(
    counts_ref, pos_ref, tile_ref, side_l_ref, side_r_ref, top_ref, bot_ref, probe_ref, intensity_ref, tables_ref,
    gprobe_out, grad_ref,
    ext_ref, over_ref, held_ref, table_ref, shifted_ref, window_ref, terms_ref,
    mid_ref, far_ref, back_ref, gprobe_ref, sems, pattern_sems,
):
    dot = lambda a, b: jnp.dot(a, b, preferred_element_type=F32)
    low, own, high = slice(0, RIM), slice(RIM, RIM + SIDE), slice(RIM + SIDE, WIDE)
    moves = [
        (probe_ref, over_ref.at[:, 8 : 8 + SIDE]),
        (probe_ref.at[:, SIDE - 8 : SIDE], over_ref.at[:, 0:8]),
        (tile_ref, ext_ref.at[:, own, own]),
        (side_l_ref, ext_ref.at[:, own, low]),
        (side_r_ref, ext_ref.at[:, own, high]),
        (tables_ref, table_ref),
        (top_ref, ext_ref.at[:, low]),
        (bot_ref, ext_ref.at[:, high]),
    ]
    copies = [pltpu.make_async_copy(src, dst, sems.at[k]) for k, (src, dst) in enumerate(moves)]
    groups = (counts_ref[0] + UNROLL - 1) // UNROLL

    def patterns(group):
        some = pl.ds(group * UNROLL, UNROLL)
        return pltpu.make_async_copy(intensity_ref.at[some], held_ref.at[some], pattern_sems.at[group])

    for copy in copies:
        copy.start()
    lax.fori_loop(0, groups, lambda group, carry: (patterns(group).start(), carry)[1], 0)
    gprobe_ref[...] = jnp.zeros((2, SIDE, SIDE), F32)
    grad_ref[...] = jnp.zeros((2, WIDE, WIDE), F32)
    for copy in copies:
        copy.wait()

    def put(u, rows, real, imag):
        for k, part in enumerate((real + imag, real, imag)):
            terms_ref[u, 0, k, rows], terms_ref[u, 1, k, rows] = split(part)

    def three(u, left, product):
        both, first, second = (
            product(terms_ref[u, 0, k], table_ref[0, k])
            + (product(terms_ref[u, 1, k], table_ref[0, k]) + product(terms_ref[u, 0, k], table_ref[1, k]))
            for k in range(3)
        )
        left[u, :, 0:SIDE] = both - second
        left[u, :, SIDE:] = both + first

    def by_rows(u, left):
        three(u, left, lambda value, table: dot(table, value))

    def by_cols(u, left):
        three(u, left, dot)

    def one_group(group, carry):
        lanes = lambda n: lax.broadcasted_iota(jnp.int32, (n, RIM), 1)
        first_rows = lax.broadcasted_iota(jnp.int32, (8, RIM), 0)
        slots = [group * UNROLL + u for u in range(UNROLL)]
        alive = [s < counts_ref[0] for s in slots]
        live = [jnp.where(a, 1.0, 0.0).astype(F32) for a in alive]
        row = [jnp.where(a, pos_ref[2 * s], 0) + RIM for s, a in zip(slots, alive)]
        col = [jnp.where(a, pos_ref[2 * s + 1], 0) + RIM for s, a in zip(slots, alive)]
        down = [r & 7 for r in row]
        right = [c & (RIM - 1) for c in col]
        row = [pl.multiple_of(r - d, 8) for r, d in zip(row, down)]
        col = [pl.multiple_of(c - d, RIM) for c, d in zip(col, right)]
        strips = [[pl.ds(pl.multiple_of(c + k * RIM, RIM), RIM) for k in range(3)] for c in col]
        pieces = [(0, 8)] + [(8, STEP - 8)] + [(k, STEP) for k in range(STEP, SIDE, STEP)]

        def at(u, start, count):
            return pl.ds(pl.multiple_of(row[u] + start, 8), count)

        for u in range(UNROLL):
            for start, count in pieces:
                rows = slice(start, start + count)
                for c in range(2):
                    three = [ext_ref[c, at(u, start, count), strip] for strip in strips[u]]
                    if start == 0:
                        wrapped = [ext_ref[c, at(u, SIDE, 8), strip] for strip in strips[u]]
                        three = [jnp.where(first_rows >= down[u], a, b) for a, b in zip(three, wrapped)]
                    window_ref[u, c, rows, 0:RIM] = jnp.where(lanes(count) >= right[u], three[0], three[2])
                    window_ref[u, c, rows, RIM:] = three[1]
            for rows in BLOCKS:
                for c in range(2):
                    turned = pltpu.roll(over_ref[c, rows.start : rows.stop + 8], STEP + down[u], 0)[0:STEP]
                    shifted_ref[u, c, rows] = pltpu.roll(turned, right[u], 1)
                pr, pi = shifted_ref[u, 0, rows], shifted_ref[u, 1, rows]
                wr, wi = window_ref[u, 0, rows], window_ref[u, 1, rows]
                put(u, rows, pr * wr - pi * wi, pr * wi + pi * wr)
            by_rows(u, mid_ref)
        for u in range(UNROLL):
            for rows in BLOCKS:
                put(u, rows, mid_ref[u, rows, 0:SIDE], mid_ref[u, rows, SIDE:])
            by_cols(u, far_ref)
        patterns(group).wait()
        for u in range(UNROLL):
            for rows in BLOCKS:
                far_real, far_imag = far_ref[u, rows, 0:SIDE], far_ref[u, rows, SIDE:]
                misfit = far_real * far_real + far_imag * far_imag - held_ref[slots[u], rows]
                misfit = misfit * live[u]
                put(u, rows, misfit * far_real, -misfit * far_imag)
            by_cols(u, mid_ref)
        for u in range(UNROLL):
            for rows in BLOCKS:
                put(u, rows, mid_ref[u, rows, 0:SIDE], mid_ref[u, rows, SIDE:])
            by_rows(u, mid_ref)
        for u in range(UNROLL):
            for start, count in pieces:
                rows = slice(start, start + count)
                br, bi = mid_ref[u, rows, 0:SIDE], -mid_ref[u, rows, SIDE:]
                pr, pi = shifted_ref[u, 0, rows], shifted_ref[u, 1, rows]
                wr, wi = window_ref[u, 0, rows], window_ref[u, 1, rows]
                here = lanes(count) >= right[u]
                for c, grad in enumerate((pr * br + pi * bi, pr * bi - pi * br)):
                    left_part = grad[:, 0:RIM]
                    three = [jnp.where(here, left_part, 0.0), grad[:, RIM:], jnp.where(here, 0.0, left_part)]
                    for part, strip in zip(three, strips[u]):
                        if start == 0:
                            near = first_rows >= down[u]
                            grad_ref[c, at(u, SIDE, 8), strip] += jnp.where(near, 0.0, part)
                            part = jnp.where(near, part, 0.0)
                        grad_ref[c, at(u, start, count), strip] += part
                for c, grad in enumerate((wr * br + wi * bi, wr * bi - wi * br)):
                    back_ref[u, c, rows] = grad
                    if start == 0:
                        back_ref[u, c, SIDE : SIDE + 8] = grad
            for rows in BLOCKS:
                for c in range(2):
                    back = jnp.where(down[u] == 0, 0, STEP + 8 - down[u])
                    turned = pltpu.roll(back_ref[u, c, rows.start : rows.stop + 8], back, 0)[0:STEP]
                    gprobe_ref[c, rows] += pltpu.roll(turned, (SIDE - right[u]) & (SIDE - 1), 1)
        return carry

    lax.fori_loop(0, groups, one_group, 0)
    copy = pltpu.make_async_copy(gprobe_ref, gprobe_out, sems.at[0])
    copy.start()
    copy.wait()


def all_slots(counts, positions, *arrays):
    smem = pl.BlockSpec(memory_space=pltpu.SMEM)
    anywhere = pl.BlockSpec(memory_space=pl.ANY)
    return pl.pallas_call(
        slots_kernel,
        out_shape=[
            jax.ShapeDtypeStruct((2, SIDE, SIDE), F32),
            jax.ShapeDtypeStruct((2, WIDE, WIDE), F32),
        ],
        in_specs=[smem, smem] + [anywhere] * len(arrays),
        out_specs=[anywhere, pl.BlockSpec(memory_space=pltpu.VMEM)],
        scratch_shapes=[
            pltpu.VMEM((2, WIDE, WIDE), F32),
            pltpu.VMEM((2, SIDE + 8, SIDE), F32),
            pltpu.VMEM((6, SIDE, SIDE), F32),
            pltpu.VMEM((2, 3, SIDE, SIDE), BF16),
            pltpu.VMEM((UNROLL, 2, SIDE, SIDE), F32),
            pltpu.VMEM((UNROLL, 2, SIDE, SIDE), F32),
            pltpu.VMEM((UNROLL, 2, 3, SIDE, SIDE), BF16),
            pltpu.VMEM((UNROLL, SIDE, WIDE), F32),
            pltpu.VMEM((UNROLL, SIDE, WIDE), F32),
            pltpu.VMEM((UNROLL, 2, SIDE + 8, SIDE), F32),
            pltpu.VMEM((2, SIDE, SIDE), F32),
            pltpu.SemaphoreType.DMA((8,)),
            pltpu.SemaphoreType.DMA((6 // UNROLL,)),
        ],
        compiler_params=pltpu.CompilerParams(vmem_limit_bytes=VMEM_BYTES),
        cost_estimate=pl.CostEstimate(flops=10_000_000_000, bytes_accessed=20_000_000, transcendentals=0),
    )(counts, positions, *arrays)


def shifted(block, axes, distance):
    count = lax.axis_size(axes)
    route = [(i, i + distance) for i in range(count) if 0 <= i + distance < count]
    return lax.ppermute(block, axes, route)


def swap(pieces, axes):
    return lax.all_to_all(pieces, axes, split_axis=0, concat_axis=0, tiled=True)


def spread(block, axes):
    count = lax.axis_size(axes)
    return swap(jnp.broadcast_to(block[None], (count,) + block.shape), axes)


def summed_everywhere(grad, scale):
    count = lax.axis_size(PLANE)
    pieces = swap(grad.reshape(count, 2 * SIDE // count, SIDE), PLANE)
    part = spread(jnp.sum(pieces, axis=0), DEEP)
    half = spread(jnp.sum(part, axis=0) * scale, FLOOR)
    return lax.all_gather(half, "core", axis=0, tiled=True).reshape(2, SIDE, SIDE)


def shards(object_field, probe_field, intensity, positions, counts):
    tables = [jnp.asarray(t) for t in spectral_tables()]
    side_l = shifted(object_field[:, :, RIM:], COL, 1)
    side_r = shifted(object_field[:, :, :RIM], COL, -1)
    middle = jnp.concatenate([side_l, object_field, side_r], axis=2)
    top = shifted(middle[:, RIM:], ROW, 1)
    bottom = shifted(middle[:, :RIM], ROW, -1)
    grad_probe, grad_wide = all_slots(
        counts.reshape(1),
        positions.reshape(-1),
        object_field,
        side_l,
        side_r,
        top,
        bottom,
        probe_field,
        intensity[0, 0],
        *tables,
    )
    from_above = shifted(grad_wide[:, RIM + SIDE :], ROW, 1)
    from_below = shifted(grad_wide[:, :RIM], ROW, -1)
    total_slots = lax.axis_size(ROW) * lax.axis_size(COL) * positions.shape[2]
    probe_update = summed_everywhere(grad_probe, 1.0 / math.sqrt(total_slots))
    rows = grad_wide[:, RIM : RIM + SIDE] + jnp.concatenate([from_above, from_below], axis=1)
    from_left = shifted(rows[:, :, RIM + SIDE :], COL, 1)
    from_right = shifted(rows[:, :, :RIM], COL, -1)
    gathered = rows[:, :, RIM : RIM + SIDE] + jnp.concatenate([from_left, from_right], axis=2)
    object_new = object_field - OBJECT_RATE * gathered
    return (object_new, probe_update)


def solution(mesh):
    chips = Mesh(mesh.devices.reshape(2, 4, 2, 16, 2), ("yh", "x", "core", "z", "yl"))
    placed = (
        P(None, ROW, COL),
        P(),
        P(ROW, COL, None, None, None),
        P(ROW, COL, None, None),
        P(ROW, COL),
    )
    return jax.shard_map(
        shards, mesh=chips, in_specs=placed, out_specs=(P(None, ROW, COL), P()), check_vma=False
    )
```

```python
import math

import jax
import jax.numpy as jnp
import ml_dtypes
import numpy as np
from jax import lax
from jax.experimental import pallas as pl
from jax.experimental.pallas import tpu as pltpu
from jax.sharding import Mesh, PartitionSpec as P

OBJECT_RATE = 0.5
ROW = ("yh", "x", "core")
COL = ("z", "yl")
PLANE = ("core", "yh", "x", "yl")
FLOOR = ("yh", "x", "yl")
DEEP = "z"
SIDE = 256
RIM = 128
WIDE = 2 * SIDE
F32 = jnp.float32
BF16 = jnp.bfloat16


def two_terms(table):
    high = table.astype(np.float32).astype(ml_dtypes.bfloat16)
    low = (table - high.astype(np.float64)).astype(np.float32).astype(ml_dtypes.bfloat16)
    return high, low


def spectral_tables():
    index = np.arange(SIDE)
    angles = (index[:, None] * index[None, :] % SIDE) * (2.0 * math.pi / SIDE)
    cos, sin = np.cos(angles) / 16.0, np.sin(angles) / 16.0
    high, low = two_terms(np.stack([cos, -sin - cos, cos - sin]))
    return (np.stack([high, low]),)


def split(value):
    high = value.astype(BF16)
    low = (value - high.astype(F32)).astype(BF16)
    return high, low


UNROLL = 3
STEP = 64
BLOCKS = [slice(k, k + STEP) for k in range(0, SIDE, STEP)]
VMEM_BYTES = 50 * 1024 * 1024


def slots_kernel(
    counts_ref, pos_ref, tile_ref, side_l_ref, side_r_ref, top_ref, bot_ref, probe_ref, intensity_ref, tables_ref,
    gprobe_out, gtop_out, gbot_out, gmid_out,
    ext_ref, over_ref, held_ref, table_ref, shifted_ref, window_ref, terms_ref,
    mid_ref, far_ref, back_ref, grad_ref, gprobe_ref, sems, pattern_sems,
):
    dot = lambda a, b: jnp.dot(a, b, preferred_element_type=F32)
    low, own, high = slice(0, RIM), slice(RIM, RIM + SIDE), slice(RIM + SIDE, WIDE)
    moves = [
        (probe_ref, over_ref.at[:, 8 : 8 + SIDE]),
        (probe_ref.at[:, SIDE - 8 : SIDE], over_ref.at[:, 0:8]),
        (tile_ref, ext_ref.at[:, own, own]),
        (side_l_ref, ext_ref.at[:, own, low]),
        (side_r_ref, ext_ref.at[:, own, high]),
        (tables_ref, table_ref),
        (top_ref, ext_ref.at[:, low]),
        (bot_ref, ext_ref.at[:, high]),
    ]
    copies = [pltpu.make_async_copy(src, dst, sems.at[k]) for k, (src, dst) in enumerate(moves)]
    groups = (counts_ref[0] + UNROLL - 1) // UNROLL

    def patterns(group):
        some = pl.ds(group * UNROLL, UNROLL)
        return pltpu.make_async_copy(intensity_ref.at[some], held_ref.at[some], pattern_sems.at[group])

    for copy in copies:
        copy.start()
    lax.fori_loop(0, groups, lambda group, carry: (patterns(group).start(), carry)[1], 0)
    gprobe_ref[...] = jnp.zeros((2, SIDE, SIDE), F32)
    grad_ref[...] = jnp.zeros((2, WIDE, WIDE), F32)
    for copy in copies:
        copy.wait()

    def put(u, rows, real, imag):
        for k, part in enumerate((real + imag, real, imag)):
            terms_ref[u, 0, k, rows], terms_ref[u, 1, k, rows] = split(part)

    def three(u, left, product):
        both, first, second = (
            product(terms_ref[u, 0, k], table_ref[0, k])
            + (product(terms_ref[u, 1, k], table_ref[0, k]) + product(terms_ref[u, 0, k], table_ref[1, k]))
            for k in range(3)
        )
        left[u, :, 0:SIDE] = both - second
        left[u, :, SIDE:] = both + first

    def by_rows(u, left):
        three(u, left, lambda value, table: dot(table, value))

    def by_cols(u, left):
        three(u, left, dot)

    def one_group(group, carry):
        lanes = lambda n: lax.broadcasted_iota(jnp.int32, (n, RIM), 1)
        first_rows = lax.broadcasted_iota(jnp.int32, (8, RIM), 0)
        slots = [group * UNROLL + u for u in range(UNROLL)]
        alive = [s < counts_ref[0] for s in slots]
        live = [jnp.where(a, 1.0, 0.0).astype(F32) for a in alive]
        row = [jnp.where(a, pos_ref[2 * s], 0) + RIM for s, a in zip(slots, alive)]
        col = [jnp.where(a, pos_ref[2 * s + 1], 0) + RIM for s, a in zip(slots, alive)]
        down = [r & 7 for r in row]
        right = [c & (RIM - 1) for c in col]
        row = [pl.multiple_of(r - d, 8) for r, d in zip(row, down)]
        col = [pl.multiple_of(c - d, RIM) for c, d in zip(col, right)]
        strips = [[pl.ds(pl.multiple_of(c + k * RIM, RIM), RIM) for k in range(3)] for c in col]
        pieces = [(0, 8)] + [(8, STEP - 8)] + [(k, STEP) for k in range(STEP, SIDE, STEP)]

        def at(u, start, count):
            return pl.ds(pl.multiple_of(row[u] + start, 8), count)

        for u in range(UNROLL):
            for start, count in pieces:
                rows = slice(start, start + count)
                for c in range(2):
                    three = [ext_ref[c, at(u, start, count), strip] for strip in strips[u]]
                    if start == 0:
                        wrapped = [ext_ref[c, at(u, SIDE, 8), strip] for strip in strips[u]]
                        three = [jnp.where(first_rows >= down[u], a, b) for a, b in zip(three, wrapped)]
                    window_ref[u, c, rows, 0:RIM] = jnp.where(lanes(count) >= right[u], three[0], three[2])
                    window_ref[u, c, rows, RIM:] = three[1]
            for rows in BLOCKS:
                for c in range(2):
                    turned = pltpu.roll(over_ref[c, rows.start : rows.stop + 8], STEP + down[u], 0)[0:STEP]
                    shifted_ref[u, c, rows] = pltpu.roll(turned, right[u], 1)
                pr, pi = shifted_ref[u, 0, rows], shifted_ref[u, 1, rows]
                wr, wi = window_ref[u, 0, rows], window_ref[u, 1, rows]
                put(u, rows, pr * wr - pi * wi, pr * wi + pi * wr)
            by_rows(u, mid_ref)
        for u in range(UNROLL):
            for rows in BLOCKS:
                put(u, rows, mid_ref[u, rows, 0:SIDE], mid_ref[u, rows, SIDE:])
            by_cols(u, far_ref)
        patterns(group).wait()
        for u in range(UNROLL):
            for rows in BLOCKS:
                far_real, far_imag = far_ref[u, rows, 0:SIDE], far_ref[u, rows, SIDE:]
                misfit = far_real * far_real + far_imag * far_imag - held_ref[slots[u], rows]
                misfit = misfit * live[u]
                put(u, rows, misfit * far_real, -misfit * far_imag)
            by_cols(u, mid_ref)
        for u in range(UNROLL):
            for rows in BLOCKS:
                put(u, rows, mid_ref[u, rows, 0:SIDE], mid_ref[u, rows, SIDE:])
            by_rows(u, mid_ref)
        for u in range(UNROLL):
            for start, count in pieces:
                rows = slice(start, start + count)
                br, bi = mid_ref[u, rows, 0:SIDE], -mid_ref[u, rows, SIDE:]
                pr, pi = shifted_ref[u, 0, rows], shifted_ref[u, 1, rows]
                wr, wi = window_ref[u, 0, rows], window_ref[u, 1, rows]
                here = lanes(count) >= right[u]
                for c, grad in enumerate((pr * br + pi * bi, pr * bi - pi * br)):
                    left_part = grad[:, 0:RIM]
                    three = [jnp.where(here, left_part, 0.0), grad[:, RIM:], jnp.where(here, 0.0, left_part)]
                    for part, strip in zip(three, strips[u]):
                        if start == 0:
                            near = first_rows >= down[u]
                            grad_ref[c, at(u, SIDE, 8), strip] += jnp.where(near, 0.0, part)
                            part = jnp.where(near, part, 0.0)
                        grad_ref[c, at(u, start, count), strip] += part
                for c, grad in enumerate((wr * br + wi * bi, wr * bi - wi * br)):
                    back_ref[u, c, rows] = grad
                    if start == 0:
                        back_ref[u, c, SIDE : SIDE + 8] = grad
            for rows in BLOCKS:
                for c in range(2):
                    back = jnp.where(down[u] == 0, 0, STEP + 8 - down[u])
                    turned = pltpu.roll(back_ref[u, c, rows.start : rows.stop + 8], back, 0)[0:STEP]
                    gprobe_ref[c, rows] += pltpu.roll(turned, (SIDE - right[u]) & (SIDE - 1), 1)
        return carry

    lax.fori_loop(0, groups, one_group, 0)
    moves = [
        (gprobe_ref, gprobe_out),
        (grad_ref.at[:, low], gtop_out),
        (grad_ref.at[:, high], gbot_out),
        (grad_ref.at[:, own], gmid_out),
    ]
    copies = [pltpu.make_async_copy(src, dst, sems.at[k]) for k, (src, dst) in enumerate(moves)]
    for copy in copies:
        copy.start()
    for copy in copies:
        copy.wait()


def all_slots(counts, positions, *arrays):
    smem = pl.BlockSpec(memory_space=pltpu.SMEM)
    anywhere = pl.BlockSpec(memory_space=pl.ANY)
    return pl.pallas_call(
        slots_kernel,
        out_shape=[
            jax.ShapeDtypeStruct((2, SIDE, SIDE), F32),
            jax.ShapeDtypeStruct((2, RIM, WIDE), F32),
            jax.ShapeDtypeStruct((2, RIM, WIDE), F32),
            jax.ShapeDtypeStruct((2, SIDE, WIDE), F32),
        ],
        in_specs=[smem, smem] + [anywhere] * len(arrays),
        out_specs=[anywhere] * 4,
        scratch_shapes=[
            pltpu.VMEM((2, WIDE, WIDE), F32),
            pltpu.VMEM((2, SIDE + 8, SIDE), F32),
            pltpu.VMEM((6, SIDE, SIDE), F32),
            pltpu.VMEM((2, 3, SIDE, SIDE), BF16),
            pltpu.VMEM((UNROLL, 2, SIDE, SIDE), F32),
            pltpu.VMEM((UNROLL, 2, SIDE, SIDE), F32),
            pltpu.VMEM((UNROLL, 2, 3, SIDE, SIDE), BF16),
            pltpu.VMEM((UNROLL, SIDE, WIDE), F32),
            pltpu.VMEM((UNROLL, SIDE, WIDE), F32),
            pltpu.VMEM((UNROLL, 2, SIDE + 8, SIDE), F32),
            pltpu.VMEM((2, WIDE, WIDE), F32),
            pltpu.VMEM((2, SIDE, SIDE), F32),
            pltpu.SemaphoreType.DMA((8,)),
            pltpu.SemaphoreType.DMA((6 // UNROLL,)),
        ],
        compiler_params=pltpu.CompilerParams(vmem_limit_bytes=VMEM_BYTES),
        cost_estimate=pl.CostEstimate(flops=10_000_000_000, bytes_accessed=20_000_000, transcendentals=0),
    )(counts, positions, *arrays)


def shifted(block, axes, distance):
    count = lax.axis_size(axes)
    route = [(i, i + distance) for i in range(count) if 0 <= i + distance < count]
    return lax.ppermute(block, axes, route)


def swap(pieces, axes):
    return lax.all_to_all(pieces, axes, split_axis=0, concat_axis=0, tiled=True)


def spread(block, axes):
    count = lax.axis_size(axes)
    return swap(jnp.broadcast_to(block[None], (count,) + block.shape), axes)


def summed_everywhere(grad, scale):
    count = lax.axis_size(PLANE)
    pieces = swap(grad.reshape(count, 2 * SIDE // count, SIDE), PLANE)
    part = spread(jnp.sum(pieces, axis=0), DEEP)
    half = spread(jnp.sum(part, axis=0) * scale, FLOOR)
    return lax.all_gather(half, "core", axis=0, tiled=True).reshape(2, SIDE, SIDE)


def shards(object_field, probe_field, intensity, positions, counts):
    tables = [jnp.asarray(t) for t in spectral_tables()]
    side_l = shifted(object_field[:, :, RIM:], COL, 1)
    side_r = shifted(object_field[:, :, :RIM], COL, -1)
    middle = jnp.concatenate([side_l, object_field, side_r], axis=2)
    top = shifted(middle[:, RIM:], ROW, 1)
    bottom = shifted(middle[:, :RIM], ROW, -1)
    grad_probe, grad_top, grad_bottom, grad_mid = all_slots(
        counts.reshape(1),
        positions.reshape(-1),
        object_field,
        side_l,
        side_r,
        top,
        bottom,
        probe_field,
        intensity[0, 0],
        *tables,
    )
    from_above = shifted(grad_bottom, ROW, 1)
    from_below = shifted(grad_top, ROW, -1)
    total_slots = lax.axis_size(ROW) * lax.axis_size(COL) * positions.shape[2]
    probe_update = summed_everywhere(grad_probe, 1.0 / math.sqrt(total_slots))
    rows = grad_mid + jnp.concatenate([from_above, from_below], axis=1)
    from_left = shifted(rows[:, :, RIM + SIDE :], COL, 1)
    from_right = shifted(rows[:, :, :RIM], COL, -1)
    gathered = rows[:, :, RIM : RIM + SIDE] + jnp.concatenate([from_left, from_right], axis=2)
    object_new = object_field - OBJECT_RATE * gathered
    return (object_new, probe_update)


def solution(mesh):
    chips = Mesh(mesh.devices.reshape(2, 4, 2, 16, 2), ("yh", "x", "core", "z", "yl"))
    placed = (
        P(None, ROW, COL),
        P(),
        P(ROW, COL, None, None, None),
        P(ROW, COL, None, None),
        P(ROW, COL),
    )
    return jax.shard_map(
        shards, mesh=chips, in_specs=placed, out_specs=(P(None, ROW, COL), P()), check_vma=False
    )
```
